32 devices in a mesh: section: 2 (over core), group: 4 (over z), rep: 4 (over y, x).
Axes of the slice: x: 2, y: 2, z: 4, core: 2. Of those that a mesh axis runs over, the one named last changes fastest.
Arguments:
- latents: bfloat16 [32, 256, 384], P(('group', 'rep')), may hold values from -6 to 6
- cond: float32 [32, 384], P(('group', 'rep')), may hold values from -6 to 6
- cotangent: bfloat16 [32, 256, 384], P(('group', 'rep')), may hold values from -6 to 6
- live_count: int32 [16, 2], P(('group', 'rep')), may hold values from 0 to 1, as said below
- adaptive_weight: bfloat16 [2, 384, 2304], P('section', 'group'), may hold values from -0.3125 to 0.3125
- adaptive_bias: bfloat16 [2, 2304], P('section', 'group'), may hold values from 0.5 to 1.5
- query_key_value_weight: bfloat16 [2, 384, 1152], P('section', 'group'), may hold values from -0.15625 to 0.15625
- output_projection_weight: bfloat16 [2, 384, 384], P('section', 'group'), may hold values from -1.25 to 1.25
- first_dense_weight: bfloat16 [2, 384, 1536], P('section', 'group'), may hold values from -0.3125 to 0.3125
- first_dense_bias: bfloat16 [2, 1536], P('section', 'group'), may hold values from -3 to 3
- second_dense_weight: bfloat16 [2, 1536, 384], P('section', 'group'), may hold values from -0.15625 to 0.15625
Outputs:
- section_outputs: bfloat16 [2, 32, 256, 384], P('section', ('group', 'rep'))
- input_grads: float32 [2, 32, 256, 384], P('section', ('group', 'rep'))
- cond_grads: float32 [2, 32, 384], P('section', ('group', 'rep'))
- grad_ada: float32 [2, 384, 2304], P('section', 'group')
- grad_bada: float32 [2, 2304], P('section', 'group')
- grad_qkv: float32 [2, 384, 1152], P('section', 'group')
- grad_proj: float32 [2, 384, 384], P('section', 'group')
- grad_fc1: float32 [2, 384, 1536], P('section', 'group')
- grad_bfc1: float32 [2, 1536], P('section', 'group')
- grad_fc2: float32 [2, 1536, 384], P('section', 'group')
The draws below stay inside these ranges and needn't reach their ends.
Inputs may be any that keep to these rules, and one draw needn't show every extreme that they name: live_count of a device block and micro-batch counts the real latents, which fill its first slots; the rest hold no latent. In every micro-batch one device block has 1 and another has none.
All inputs are finite; a program needn't handle non-finite values.
Results may differ from the reference program's by a relative error of at most 0.018.
Values may be sent and summed in bfloat16 or wider, within the bound.
A program may use at most 192 MiB of HBM per device.

```python
import math
import jax
import jax.numpy as jnp
from jax import lax

D = 384
HEADS = 6
HEAD_DIM = 64
FF = 1536
TOK = 256
MB = 2
SLOTS = 1
DATA_DEV = 16
LATENTS = 32


def draw_live_count(key, part):
    key = jax.random.fold_in(key, 11)
    key_counts = jax.random.fold_in(key, 1)
    key_spot = jax.random.fold_in(key, 2)
    counts = jax.random.randint(key_counts, (DATA_DEV, MB), 0, SLOTS + 1)
    spot = jax.random.randint(key_spot, (MB,), 0, DATA_DEV)
    rows = jnp.arange(DATA_DEV, dtype=jnp.int32)[:, None]
    counts = jnp.where(rows == spot[None, :], SLOTS, counts)
    counts = jnp.where(rows == (spot[None, :] + 1) % DATA_DEV, 0, counts)
    return counts.astype(jnp.int32)


def level_of(rng, extent, cuts, least, top_value):
    def one(axis_at, blocks):
        steps = jax.random.uniform(jax.random.fold_in(jax.random.fold_in(rng, 6), axis_at), (blocks,), jnp.float32, least / len(cuts), top_value / len(cuts))
        return jnp.repeat(jnp.exp(steps), extent[axis_at] // blocks).reshape((-1,) + (1,) * (len(extent) - axis_at - 1))

    level = one(*cuts[0])
    for cut in cuts[1:]:
        level = level * one(*cut)
    return level


def bell_draw(own_key, shape, scale, limit, cuts=(), kind=jnp.bfloat16):
    result = scale * jax.random.normal(own_key, shape, jnp.float32)
    if cuts:
        result = result * level_of(own_key, shape, cuts, -0.22, 0.18)
    return jnp.clip(result, -limit, limit).astype(kind)


def setup_inputs(seed: int = 0) -> dict:
    key_list = jax.random.split(jax.random.key(seed), 12)
    latents = bell_draw(key_list[0], (LATENTS, TOK, D), 1.0, 6.0, ((0, 16),))
    cond = bell_draw(key_list[1], (LATENTS, D), 1.0, 6.0, ((0, 16),), jnp.float32)
    cotangent = bell_draw(key_list[2], (LATENTS, TOK, D), 1.0, 6.0, ((0, 16),))
    live_count = draw_live_count(jax.random.fold_in(key_list[11], 71), 0)
    adaptive_weight = bell_draw(key_list[4], (2, D, 6 * D), D ** -0.5, 0.3125, ((0, 2), (1, 4)))
    adaptive_bias = jnp.clip(0.5 + 1.0 * jax.random.uniform(key_list[5], (2, 6 * D), jnp.float32) ** level_of(key_list[5], (2, 6 * D), ((0, 2), (1, 4)), -0.2, 0.2), 0.5, 1.5).astype(jnp.bfloat16)
    query_key_value_weight = bell_draw(key_list[6], (2, D, 3 * D), (4 * D) ** -0.5, 0.15625, ((0, 2), (1, 4)))
    output_projection_weight = bell_draw(key_list[7], (2, D, D), (D // 16) ** -0.5, 1.25, ((0, 2), (1, 4)))
    first_dense_weight = bell_draw(key_list[8], (2, D, FF), D ** -0.5, 0.3125, ((0, 2), (1, 4)))
    first_dense_bias = bell_draw(key_list[9], (2, FF), 0.5, 3.0, ((0, 2), (1, 4)))
    second_dense_weight = bell_draw(key_list[10], (2, FF, D), FF ** -0.5, 0.15625, ((0, 2), (1, 4)))
    return {"latents": latents, "cond": cond, "cotangent": cotangent, "live_count": live_count, "adaptive_weight": adaptive_weight, "adaptive_bias": adaptive_bias, "query_key_value_weight": query_key_value_weight, "output_projection_weight": output_projection_weight, "first_dense_weight": first_dense_weight, "first_dense_bias": first_dense_bias, "second_dense_weight": second_dense_weight}


epsilon = 1e-06

@jax.custom_vjp
def reduced_precision(v):
    return lax.optimization_barrier(v.astype(jnp.bfloat16)).astype(jnp.float32)

@jax.custom_vjp
def reduced_backward(v):
    return v

def low_keep(v):
    return (reduced_precision(v), None)

def low_pass(kept, grad):
    return (grad,)

def back_keep(v):
    return (v, None)

def back_low(kept, grad):
    return (reduced_precision(grad),)
reduced_precision.defvjp(low_keep, low_pass)
reduced_backward.defvjp(back_keep, back_low)

def product(left_side, right_side):
    return jnp.einsum('...d,de->...e', left_side, right_side, precision=lax.Precision.HIGHEST)

def normalize(values):
    center = values - lax.optimization_barrier(jnp.mean(values, axis=-1, keepdims=True))
    spread = lax.optimization_barrier(jnp.mean(center * center, axis=-1, keepdims=True))
    return center * lax.rsqrt(spread + epsilon)

def diffusion_transformer_block(input_rows, condition_vector, adaptive_weight, adaptive_bias, query_key_value_weight, output_projection_weight, first_dense_weight, first_dense_bias, second_dense_weight):
    count, length = (input_rows.shape[0], input_rows.shape[1])
    modulation = reduced_backward(product(reduced_precision(jax.nn.silu(condition_vector)), adaptive_weight) + adaptive_bias)
    shift_attn, scale_attn, gate_attn, shift_mlp, scale_mlp, gate_mlp = jnp.split(modulation, 6, axis=-1)
    normed = reduced_precision(normalize(input_rows) * (1.0 + scale_attn[:, None, :]) + shift_attn[:, None, :])
    triple = reduced_backward(reduced_precision(product(normed, query_key_value_weight)))
    queries = triple[..., :D].reshape(count, length, HEADS, HEAD_DIM)
    keys_part = triple[..., D:2 * D].reshape(count, length, HEADS, HEAD_DIM)
    values_part = triple[..., 2 * D:].reshape(count, length, HEADS, HEAD_DIM)
    scores = jnp.einsum('snhe,smhe->shnm', queries, keys_part, precision=lax.Precision.HIGHEST)
    scores = reduced_backward(scores * HEAD_DIM ** (-0.5))
    probs = reduced_precision(jax.nn.softmax(scores, axis=-1))
    mixed = jnp.einsum('shnm,smhe->snhe', probs, values_part, precision=lax.Precision.HIGHEST)
    mixed = reduced_backward(reduced_precision(mixed.reshape(count, length, D)))
    attended = reduced_backward(product(mixed, output_projection_weight))
    middle = input_rows + gate_attn[:, None, :] * attended
    second = reduced_precision(normalize(middle) * (1.0 + scale_mlp[:, None, :]) + shift_mlp[:, None, :])
    hidden = reduced_backward(product(second, first_dense_weight) + first_dense_bias)
    activated = reduced_precision(jax.nn.gelu(hidden, approximate=True))
    branch = reduced_backward(product(activated, second_dense_weight))
    return middle + gate_mlp[:, None, :] * branch

def relay(input_rows, condition_vector, test_rows, test_condition, leading_weights, trailing_weights):
    handed_over = reduced_backward(reduced_precision(diffusion_transformer_block(input_rows, condition_vector, *leading_weights)) + test_rows)
    final_result = diffusion_transformer_block(handed_over, reduced_backward(condition_vector + test_condition), *trailing_weights)
    return (handed_over, final_result)

def reference(latents, cond, cotangent, live_count, adaptive_weight, adaptive_bias, query_key_value_weight, output_projection_weight, first_dense_weight, first_dense_bias, second_dense_weight):
    stacked = tuple((array.astype(jnp.float32) for array in (adaptive_weight, adaptive_bias, query_key_value_weight, output_projection_weight, first_dense_weight, first_dense_bias, second_dense_weight)))
    leading_weights = tuple((array[0] for array in stacked))
    trailing_weights = tuple((array[1] for array in stacked))
    position = jnp.arange(LATENTS, dtype=jnp.int32)
    device = position // (MB * SLOTS)
    batch = position // SLOTS % MB
    within = position % SLOTS
    live = (within < live_count[device, batch]).astype(jnp.float32)
    block_size = math.gcd(LATENTS, max(1, 4096 // TOK))
    blocks = LATENTS // block_size

    def split_rows(array):
        return array.reshape((blocks, block_size) + array.shape[1:])

    def visit(carry, pieces):
        input_rows, condition_vector, tangent, alive = pieces
        input_rows = input_rows.astype(jnp.float32)
        condition_vector = condition_vector.astype(jnp.float32)
        tangent = tangent.astype(jnp.float32) * alive[:, None, None]
        outputs, pullback = jax.vjp(relay, input_rows, condition_vector, jnp.zeros_like(input_rows), jnp.zeros_like(condition_vector), leading_weights, trailing_weights)
        grads = pullback((jnp.zeros_like(outputs[0]), tangent))
        d_inputs, d_cond, d_handed, d_probe, d_first, d_second = grads
        carry = jax.tree.map(lambda former, latter: former + latter, carry, (d_first, d_second))
        handed_out = (outputs[0] * alive[:, None, None]).astype(jnp.bfloat16)
        final_out = (outputs[1] * alive[:, None, None]).astype(jnp.bfloat16)
        return (carry, (handed_out, final_out, d_inputs, d_handed, d_cond, d_probe))
    start = jax.tree.map(jnp.zeros_like, (leading_weights, trailing_weights))
    totals, results = lax.scan(visit, start, (split_rows(latents), split_rows(cond), split_rows(cotangent), split_rows(live)))
    handed_out, final_out, d_inputs, d_handed, d_cond, d_probe = [array.reshape((LATENTS,) + array.shape[2:]) for array in results]
    section_outputs = jnp.stack([handed_out, final_out])
    input_grads = jnp.stack([d_inputs, d_handed])
    cond_grads = jnp.stack([d_cond, d_probe])
    merged = [jnp.stack([former, latter]) for former, latter in zip(totals[0], totals[1])]
    return (section_outputs, input_grads, cond_grads, merged[0], merged[1], merged[2], merged[3], merged[4], merged[5], merged[6])
```

```python
from functools import partial

import jax
import jax.numpy as jnp
from jax import lax
from jax.experimental import pallas as pl
from jax.experimental.pallas import tpu as pltpu
from jax.sharding import PartitionSpec as P

D = 384
HEADS = 6
HEAD_DIM = 64
FF = 1536
TOK = 256
EPS = 1e-06
F32 = jnp.float32
BF16 = jnp.bfloat16
NN = (((1,), (0,)), ((), ()))
NT = (((1,), (1,)), ((), ()))
TN = (((0,), (0,)), ((), ()))
GELU_A = 0.7978845608028654
GELU_B = 0.044715


def dot(a, b, dims=NN):
    return lax.dot_general(a, b, dims, preferred_element_type=F32)


def cols(j, width=D):
    return slice(j * width, (j + 1) * width)


def layer_norm(x):
    center = x - jnp.mean(x, axis=-1, keepdims=True)
    spread = jnp.mean(center * center, axis=-1, keepdims=True)
    rstd = lax.rsqrt(spread + EPS)
    return center * rstd, rstd


def layer_norm_back(grad, xhat, rstd):
    first = jnp.mean(grad, axis=-1, keepdims=True)
    second = jnp.mean(grad * xhat, axis=-1, keepdims=True)
    return rstd * (grad - first - xhat * second)


def total_rows(x):
    return jnp.sum(x, axis=0, keepdims=True)


def block_forward(s, x, mod, w8, f2, b1, kept):
    xa, ra, a_low, qkv, probs, o_low, att, xm, rm, m_low, gp, g_low, branch = kept
    xhat, rstd = layer_norm(x)
    xa[s] = xhat
    ra[s] = rstd
    a_low[s] = (xhat * (1.0 + mod[s, 1:2]) + mod[s, 0:1]).astype(BF16)
    for j in range(3):
        qkv[s, :, cols(j)] = dot(a_low[s], w8[s, j]).astype(BF16)
    for h in range(HEADS):
        q = qkv[s, :, cols(h, HEAD_DIM)] * 0.125
        k = qkv[s, :, cols(HEADS + h, HEAD_DIM)]
        v = qkv[s, :, cols(2 * HEADS + h, HEAD_DIM)]
        scores = dot(q, k, NT)
        e = jnp.exp(scores - jnp.max(scores, axis=-1, keepdims=True))
        p = (e * (1.0 / jnp.sum(e, axis=-1, keepdims=True))).astype(BF16)
        probs[s, h] = p
        o_low[s, :, cols(h, HEAD_DIM)] = dot(p, v).astype(BF16)
    attended = dot(o_low[s], w8[s, 3])
    att[s] = attended
    x1 = x + mod[s, 2:3] * attended
    xhat, rstd = layer_norm(x1)
    xm[s] = xhat
    rm[s] = rstd
    m_low[s] = (xhat * (1.0 + mod[s, 4:5]) + mod[s, 3:4]).astype(BF16)
    for j in range(4):
        u = dot(m_low[s], w8[s, 4 + j]) + b1[s, :, cols(j)]
        u2 = u * u
        t = jnp.tanh(GELU_A * u * (1.0 + GELU_B * u2))
        half = 0.5 * (1.0 + t)
        g_low[s, :, cols(j)] = (u * half).astype(BF16)
        gp[s, :, cols(j)] = half + (0.5 * GELU_A) * u * (1.0 - t * t) * (
            1.0 + (3.0 * GELU_B) * u2
        )
    r = dot(g_low[s], f2[s])
    branch[s] = r
    return x1 + mod[s, 5:6] * r


def block_backward(s, dy, mod, w8, f2, kept, g8, gf2, db1, dmod, dqkv, dulow):
    xa, ra, a_low, qkv, probs, o_low, att, xm, rm, m_low, gp, g_low, branch = kept
    dmod[s, 5:6] = total_rows(dy * branch[s])
    dr = (mod[s, 5:6] * dy).astype(BF16)
    for j in range(4):
        gf2[s, cols(j)] = dot(g_low[s, :, cols(j)], dr, TN).astype(BF16)
        du = (dot(dr, f2[s, cols(j)], NT) * gp[s, :, cols(j)]).astype(BF16)
        dulow[:, cols(j)] = du
        db1[s, :, cols(j)] = total_rows(du.astype(F32))
        g8[s, 4 + j] = dot(m_low[s], du, TN).astype(BF16)
    dm = dot(dulow[:, cols(0)], w8[s, 4], NT)
    for j in range(1, 4):
        dm = dm + dot(dulow[:, cols(j)], w8[s, 4 + j], NT)
    dmod[s, 3:4] = total_rows(dm)
    dmod[s, 4:5] = total_rows(dm * xm[s])
    dx1 = dy + layer_norm_back(dm * (1.0 + mod[s, 4:5]), xm[s], rm[s])
    dmod[s, 2:3] = total_rows(dx1 * att[s])
    datt = (mod[s, 2:3] * dx1).astype(BF16)
    g8[s, 3] = dot(o_low[s], datt, TN).astype(BF16)
    do_low = dot(datt, w8[s, 3], NT).astype(BF16)
    for h in range(HEADS):
        q = qkv[s, :, cols(h, HEAD_DIM)]
        k = qkv[s, :, cols(HEADS + h, HEAD_DIM)]
        v = qkv[s, :, cols(2 * HEADS + h, HEAD_DIM)]
        do = do_low[:, cols(h, HEAD_DIM)]
        p = probs[s, h]
        dqkv[:, cols(2 * HEADS + h, HEAD_DIM)] = dot(p, do, TN).astype(BF16)
        rowsum = jnp.sum(
            do.astype(F32) * o_low[s, :, cols(h, HEAD_DIM)].astype(F32), axis=-1, keepdims=True
        )
        ds = (p.astype(F32) * (dot(do, v, NT) - rowsum)).astype(BF16)
        dqkv[:, cols(h, HEAD_DIM)] = (dot(ds, k) * 0.125).astype(BF16)
        dqkv[:, cols(HEADS + h, HEAD_DIM)] = (dot(ds, q, TN) * 0.125).astype(BF16)
    da = None
    for j in range(3):
        part = dqkv[:, cols(j)]
        g8[s, j] = dot(a_low[s], part, TN).astype(BF16)
        term = dot(part, w8[s, j], NT)
        da = term if da is None else da + term
    dmod[s, 0:1] = total_rows(da)
    dmod[s, 1:2] = total_rows(da * xa[s])
    return dx1 + layer_norm_back(da * (1.0 + mod[s, 1:2]), xa[s], ra[s])


def relay_kernel(
    x_ref, tan_ref, live_ref, mod, b1, w8, f2,
    h_ref, z_ref, dlat_ref, dh_ref, dmod, db1, g8, gf2,
    *scratch,
):
    kept = scratch[:13]
    dqkv, dulow = scratch[13:]
    live = live_ref[...]
    h = block_forward(0, x_ref[...].astype(F32), mod, w8, f2, b1, kept).astype(BF16)
    h_ref[...] = (h.astype(F32) * live).astype(BF16)
    z = block_forward(1, h.astype(F32), mod, w8, f2, b1, kept)
    z_ref[...] = (z * live).astype(BF16)
    dy = tan_ref[...].astype(F32) * live
    dh = block_backward(1, dy, mod, w8, f2, kept, g8, gf2, db1, dmod, dqkv, dulow).astype(BF16)
    dh_ref[...] = dh
    dlat_ref[...] = block_backward(
        0, dh.astype(F32), mod, w8, f2, kept, g8, gf2, db1, dmod, dqkv, dulow
    )


def relay(x, tangent, live, mod, b1, w8, f2):
    shapes = (
        ((TOK, D), BF16),
        ((TOK, D), BF16),
        ((TOK, D), F32),
        ((TOK, D), BF16),
        ((2, 6, D), F32),
        ((2, 1, FF), F32),
        ((2, 8, D, D), BF16),
        ((2, FF, D), BF16),
    )
    keeps = (
        ((2, TOK, D), F32),
        ((2, TOK, 1), F32),
        ((2, TOK, D), BF16),
        ((2, TOK, 3 * D), BF16),
        ((2, HEADS, TOK, TOK), BF16),
        ((2, TOK, D), BF16),
        ((2, TOK, D), F32),
        ((2, TOK, D), F32),
        ((2, TOK, 1), F32),
        ((2, TOK, D), BF16),
        ((2, TOK, FF), F32),
        ((2, TOK, FF), BF16),
        ((2, TOK, D), F32),
        ((TOK, 3 * D), BF16),
        ((TOK, FF), BF16),
    )
    vmem = pl.BlockSpec(memory_space=pltpu.VMEM)
    return pl.pallas_call(
        relay_kernel,
        out_shape=[jax.ShapeDtypeStruct(*s) for s in shapes],
        in_specs=[vmem] * 7,
        out_specs=[vmem] * 8,
        scratch_shapes=[pltpu.VMEM(*s) for s in keeps],
        compiler_params=pltpu.CompilerParams(vmem_limit_bytes=56 * 2**20),
        name="relay",
    )(x, tangent, live, mod, b1, w8, f2)


def chunked(w):
    return jnp.swapaxes(w.reshape(2, D, -1, D), 1, 2)


def gather_weights(wqkv, wproj, wfc1, wfc2):
    def full(w):
        g = lax.all_gather(w, ("section", "group"), axis=0, tiled=True)
        return g.reshape(2, -1, w.shape[-1])

    w8 = jnp.concatenate([chunked(full(w)) for w in (wqkv, wproj, wfc1)], axis=1)
    return w8, full(wfc2)


def reduce_weights(g8, gf2):
    groups = lax.axis_size("group")

    def owned(g):
        g = g.reshape(2 * groups, -1, g.shape[-1])
        g = lax.psum_scatter(g, ("section", "group"), scatter_dimension=0, tiled=True)
        return lax.psum(g, "rep").astype(F32)

    def part(j, n):
        return owned(jnp.swapaxes(g8[:, j : j + n], 1, 2).reshape(2, D, n * D))

    return part(0, 3), part(3, 1), part(4, 4), owned(gf2)


def swap(value):
    return lax.ppermute(value, "section", [(0, 1), (1, 0)])


def body(
    latents, cond, cotangent, live_count,
    wada, bada, wqkv, wproj, wfc1, bfc1, wfc2,
):
    core = lax.axis_index("section")
    zi = lax.axis_index("group")
    ri = lax.axis_index("rep")
    groups = lax.axis_size("group")
    reps = lax.axis_size("rep")
    rows = D // groups
    is_first = core == 0

    def pick(a):
        return lax.dynamic_index_in_dim(a, core, 0, keepdims=False)

    live = (live_count[0] > 0).astype(F32)
    x = pick(latents)
    tangent = pick(cotangent)
    conds = lax.all_gather(cond, ("group", "rep"), axis=0, tiled=True)
    silu_all = jax.nn.silu(conds).astype(BF16)
    silu_rows = lax.dynamic_slice_in_dim(silu_all, zi * rows, rows, 1)
    biases = lax.all_gather(
        jnp.concatenate([bada, bfc1], axis=1), ("section", "group"), axis=0, tiled=True
    ).reshape(2, groups, -1)
    bias_ada = biases[..., : bada.shape[1]].reshape(2, 6 * D).astype(F32)
    b1 = biases[..., bada.shape[1] :].reshape(2, 1, FF).astype(F32)
    ours = lax.dynamic_index_in_dim(
        silu_rows.reshape(groups, reps, 2, rows), ri, 1, keepdims=False
    ).reshape(groups * 2, rows)
    partial_mod = jnp.dot(ours, wada[0], preferred_element_type=F32)
    own = lax.psum_scatter(partial_mod, "group", scatter_dimension=0, tiled=True)
    mods = lax.all_gather(own, "section", axis=0, tiled=False)
    mod = (lax.dynamic_index_in_dim(mods, core, 1, keepdims=False) + bias_ada).reshape(2, 6, D)

    w8, f2 = gather_weights(wqkv, wproj, wfc1, wfc2)
    h, z, dlat, dh, dmod, db1, g8, gf2 = relay(
        x, tangent, jnp.broadcast_to(pick(live), (1, 1)), mod, b1, w8, f2
    )

    dmod_low = dmod.reshape(2, 6 * D).astype(BF16)
    small = jnp.concatenate([dmod_low, db1.reshape(2, FF).astype(BF16)], axis=1)
    everyone = lax.all_gather(small, ("group", "rep", "section"), axis=0, tiled=False)
    mine = lax.dynamic_index_in_dim(everyone, core, 1, keepdims=False)
    dmod_all = mine[:, : 6 * D]
    grad_ada = lax.dot_general(silu_rows, dmod_all, TN, preferred_element_type=F32)
    sums = jnp.sum(mine.astype(F32), axis=0)
    wide = 6 * D // groups
    grad_bada = lax.dynamic_slice_in_dim(sums[: 6 * D], zi * wide, wide, 0)
    high = FF // groups
    grad_bfc1 = lax.dynamic_slice_in_dim(sums[6 * D :], zi * high, high, 0)
    ours = lax.dynamic_index_in_dim(
        dmod_all.reshape(groups, reps, 2, 6 * D), ri, 1, keepdims=False
    ).reshape(groups * 2, 6 * D)
    dsc_part = lax.dot_general(ours, wada[0], NT, preferred_element_type=F32)
    dsc_all = lax.all_gather(dsc_part, ("section", "group"), axis=0, tiled=False)
    dsc_all = lax.dynamic_slice_in_dim(dsc_all, 2 * zi, 2, 1)
    dsc = jnp.swapaxes(dsc_all.reshape(2, groups, 2, rows), 1, 2).reshape(2, 2, D)
    sig = jax.nn.sigmoid(cond)
    dc = dsc * (sig * (1.0 + cond * (1.0 - sig)))
    low = dc[1].astype(BF16).astype(F32)
    cond_grads = jnp.where(is_first, dc[0] + low, low)

    wq, wp, w1, w2 = reduce_weights(g8, gf2)

    sent = swap((jnp.where(is_first, z, h), jnp.where(is_first, dh, dlat.astype(BF16))))
    keep = jnp.where(is_first, h, z)
    section_outputs = jnp.where(
        is_first, jnp.stack([keep, sent[0]]), jnp.stack([sent[0], keep])
    )
    kept_grad = jnp.where(is_first, dlat, dh.astype(F32))
    got = sent[1].astype(F32)
    input_grads = jnp.where(is_first, jnp.stack([kept_grad, got]), jnp.stack([got, kept_grad]))
    return (
        section_outputs[None],
        input_grads[None],
        cond_grads[None],
        grad_ada[None],
        grad_bada[None],
        wq,
        wp,
        w1,
        grad_bfc1[None],
        w2,
    )


def solution(mesh):
    data = P(("group", "rep"))
    weight = P("section", "group")
    return jax.shard_map(
        body,
        mesh=mesh,
        in_specs=(data,) * 4 + (weight,) * 7,
        out_specs=(P("section", ("group", "rep")),) * 3 + (weight,) * 7,
        check_vma=False,
    )
```

```python
from functools import partial

import jax
import jax.numpy as jnp
from jax import lax
from jax.experimental import pallas as pl
from jax.experimental.pallas import tpu as pltpu
from jax.sharding import PartitionSpec as P

D = 384
HEADS = 6
HEAD_DIM = 64
FF = 1536
TOK = 256
EPS = 1e-06
F32 = jnp.float32
BF16 = jnp.bfloat16
NN = (((1,), (0,)), ((), ()))
NT = (((1,), (1,)), ((), ()))
TN = (((0,), (0,)), ((), ()))
GELU_A = 0.7978845608028654
GELU_B = 0.044715


def dot(a, b, dims=NN):
    return lax.dot_general(a, b, dims, preferred_element_type=F32)


def cols(j, width=D):
    return slice(j * width, (j + 1) * width)


def layer_norm(x):
    center = x - jnp.mean(x, axis=-1, keepdims=True)
    spread = jnp.mean(center * center, axis=-1, keepdims=True)
    rstd = lax.rsqrt(spread + EPS)
    return center * rstd, rstd


def layer_norm_back(grad, xhat, rstd):
    first = jnp.mean(grad, axis=-1, keepdims=True)
    second = jnp.mean(grad * xhat, axis=-1, keepdims=True)
    return rstd * (grad - first - xhat * second)


def total_rows(x):
    return jnp.sum(x, axis=0, keepdims=True)


def block_forward(s, x, mod, w8, f2, b1, kept):
    xa, ra, a_low, qkv, probs, o_low, att, xm, rm, m_low, gp, g_low, branch = kept
    xhat, rstd = layer_norm(x)
    xa[s] = xhat
    ra[s] = rstd
    a_low[s] = (xhat * (1.0 + mod[s, 1:2]) + mod[s, 0:1]).astype(BF16)
    for j in range(3):
        qkv[s, :, cols(j)] = dot(a_low[s], w8[s, j]).astype(BF16)
    for h in range(HEADS):
        q = qkv[s, :, cols(h, HEAD_DIM)] * 0.125
        k = qkv[s, :, cols(HEADS + h, HEAD_DIM)]
        v = qkv[s, :, cols(2 * HEADS + h, HEAD_DIM)]
        scores = dot(q, k, NT)
        e = jnp.exp(scores - jnp.max(scores, axis=-1, keepdims=True))
        p = (e * (1.0 / jnp.sum(e, axis=-1, keepdims=True))).astype(BF16)
        probs[s, h] = p
        o_low[s, :, cols(h, HEAD_DIM)] = dot(p, v).astype(BF16)
    attended = dot(o_low[s], w8[s, 3])
    att[s] = attended
    x1 = x + mod[s, 2:3] * attended
    xhat, rstd = layer_norm(x1)
    xm[s] = xhat
    rm[s] = rstd
    m_low[s] = (xhat * (1.0 + mod[s, 4:5]) + mod[s, 3:4]).astype(BF16)
    for j in range(4):
        u = dot(m_low[s], w8[s, 4 + j]) + b1[s, :, cols(j)]
        u2 = u * u
        t = jnp.tanh(GELU_A * u * (1.0 + GELU_B * u2))
        half = 0.5 * (1.0 + t)
        g_low[s, :, cols(j)] = (u * half).astype(BF16)
        gp[s, :, cols(j)] = half + (0.5 * GELU_A) * u * (1.0 - t * t) * (
            1.0 + (3.0 * GELU_B) * u2
        )
    r = dot(g_low[s], f2[s])
    branch[s] = r
    return x1 + mod[s, 5:6] * r


def block_backward(s, dy, mod, w8, f2, kept, g8, gf2, db1, dmod, dqkv, dulow):
    xa, ra, a_low, qkv, probs, o_low, att, xm, rm, m_low, gp, g_low, branch = kept
    dmod[s, 5:6] = total_rows(dy * branch[s])
    dr = (mod[s, 5:6] * dy).astype(BF16)
    for j in range(4):
        gf2[s, cols(j)] = dot(g_low[s, :, cols(j)], dr, TN).astype(BF16)
        du = (dot(dr, f2[s, cols(j)], NT) * gp[s, :, cols(j)]).astype(BF16)
        dulow[:, cols(j)] = du
        db1[s, :, cols(j)] = total_rows(du.astype(F32))
        g8[s, 4 + j] = dot(m_low[s], du, TN).astype(BF16)
    dm = dot(dulow[:, cols(0)], w8[s, 4], NT)
    for j in range(1, 4):
        dm = dm + dot(dulow[:, cols(j)], w8[s, 4 + j], NT)
    dmod[s, 3:4] = total_rows(dm)
    dmod[s, 4:5] = total_rows(dm * xm[s])
    dx1 = dy + layer_norm_back(dm * (1.0 + mod[s, 4:5]), xm[s], rm[s])
    dmod[s, 2:3] = total_rows(dx1 * att[s])
    datt = (mod[s, 2:3] * dx1).astype(BF16)
    g8[s, 3] = dot(o_low[s], datt, TN).astype(BF16)
    do_low = dot(datt, w8[s, 3], NT).astype(BF16)
    for h in range(HEADS):
        q = qkv[s, :, cols(h, HEAD_DIM)]
        k = qkv[s, :, cols(HEADS + h, HEAD_DIM)]
        v = qkv[s, :, cols(2 * HEADS + h, HEAD_DIM)]
        do = do_low[:, cols(h, HEAD_DIM)]
        p = probs[s, h]
        dqkv[:, cols(2 * HEADS + h, HEAD_DIM)] = dot(p, do, TN).astype(BF16)
        rowsum = jnp.sum(
            do.astype(F32) * o_low[s, :, cols(h, HEAD_DIM)].astype(F32), axis=-1, keepdims=True
        )
        ds = (p.astype(F32) * (dot(do, v, NT) - rowsum)).astype(BF16)
        dqkv[:, cols(h, HEAD_DIM)] = (dot(ds, k) * 0.125).astype(BF16)
        dqkv[:, cols(HEADS + h, HEAD_DIM)] = (dot(ds, q, TN) * 0.125).astype(BF16)
    da = None
    for j in range(3):
        part = dqkv[:, cols(j)]
        g8[s, j] = dot(a_low[s], part, TN).astype(BF16)
        term = dot(part, w8[s, j], NT)
        da = term if da is None else da + term
    dmod[s, 0:1] = total_rows(da)
    dmod[s, 1:2] = total_rows(da * xa[s])
    return dx1 + layer_norm_back(da * (1.0 + mod[s, 1:2]), xa[s], ra[s])


def relay_kernel(
    x_ref, tan_ref, live_ref, mod, b1, w8, f2,
    h_ref, z_ref, dlat_ref, dh_ref, dmod, db1, g8, gf2,
    *scratch,
):
    kept = scratch[:13]
    dqkv, dulow = scratch[13:]
    live = live_ref[...]
    h = block_forward(0, x_ref[...].astype(F32), mod, w8, f2, b1, kept).astype(BF16)
    h_ref[...] = (h.astype(F32) * live).astype(BF16)
    z = block_forward(1, h.astype(F32), mod, w8, f2, b1, kept)
    z_ref[...] = (z * live).astype(BF16)
    dy = tan_ref[...].astype(F32) * live
    dh = block_backward(1, dy, mod, w8, f2, kept, g8, gf2, db1, dmod, dqkv, dulow).astype(BF16)
    dh_ref[...] = dh
    dlat_ref[...] = block_backward(
        0, dh.astype(F32), mod, w8, f2, kept, g8, gf2, db1, dmod, dqkv, dulow
    )


def relay(x, tangent, live, mod, b1, w8, f2):
    shapes = (
        ((TOK, D), BF16),
        ((TOK, D), BF16),
        ((TOK, D), F32),
        ((TOK, D), BF16),
        ((2, 6, D), F32),
        ((2, 1, FF), F32),
        ((2, 8, D, D), BF16),
        ((2, FF, D), BF16),
    )
    keeps = (
        ((2, TOK, D), F32),
        ((2, TOK, 1), F32),
        ((2, TOK, D), BF16),
        ((2, TOK, 3 * D), BF16),
        ((2, HEADS, TOK, TOK), BF16),
        ((2, TOK, D), BF16),
        ((2, TOK, D), F32),
        ((2, TOK, D), F32),
        ((2, TOK, 1), F32),
        ((2, TOK, D), BF16),
        ((2, TOK, FF), F32),
        ((2, TOK, FF), BF16),
        ((2, TOK, D), F32),
        ((TOK, 3 * D), BF16),
        ((TOK, FF), BF16),
    )
    vmem = pl.BlockSpec(memory_space=pltpu.VMEM)
    return pl.pallas_call(
        relay_kernel,
        out_shape=[jax.ShapeDtypeStruct(*s) for s in shapes],
        in_specs=[vmem] * 7,
        out_specs=[vmem] * 8,
        scratch_shapes=[pltpu.VMEM(*s) for s in keeps],
        compiler_params=pltpu.CompilerParams(vmem_limit_bytes=56 * 2**20),
        name="relay",
    )(x, tangent, live, mod, b1, w8, f2)


MESH = pl.DeviceIdType.MESH


def places():
    core, z, r = (lax.axis_index(n) for n in ("section", "group", "rep"))
    return core, z, r, lax.axis_size("group"), lax.axis_size("rep")


def remote(src, dst, sems, target):
    return pltpu.make_async_remote_copy(
        src_ref=src,
        dst_ref=dst,
        send_sem=sems[0],
        recv_sem=sems[1],
        device_id=target,
        device_id_type=MESH,
    )


def gather_kernel(
    cond, bias, wada, wqkv, wproj, wfc1, wfc2,
    w8, f2, pin,
    condbuf, pout, lsem, csem, psem, onesem, twosem, sibsem,
):
    core, z, r, groups, reps = places()
    quarter = lax.rem(r, 4)
    base = r - quarter
    sib = 1 - core
    local = []
    for j in range(8):
        if j < 3:
            src = wqkv.at[:, cols(j)]
        elif j == 3:
            src = wproj
        else:
            src = wfc1.at[:, cols(j - 4)]
        local.append(pltpu.make_async_copy(src, w8.at[core, j, z], lsem.at[j]))
    local.append(pltpu.make_async_copy(wfc2, f2.at[core, z], lsem.at[8]))
    for copy in local:
        copy.start()

    sends = []
    for d in range(1, groups):
        to = lax.rem(z + d, groups)
        copy = remote(
            cond.at[to], condbuf.at[z], (csem.at[0, d - 1], csem.at[1, d - 1]), (core, to, r)
        )
        copy.start()
        sends.append(copy)
    condbuf[z] = cond[z]

    for copy in local:
        copy.wait()

    def piece(zz, qq):
        return w8.at[core, pl.ds(2 * qq, 2), zz], f2.at[core, zz, qq]

    def shard(cc, zz):
        return w8.at[cc, :, zz], f2.at[cc, zz]

    def both(refs, sems, target):
        return [
            remote(ref, ref, (sems(0, i), sems(1, i)), target) for i, ref in enumerate(refs)
        ]

    def one(d, zz, target):
        return both(piece(zz, quarter), lambda k, i: onesem.at[k, d - 1, i], target)

    def two(d, e, zz, qq, target):
        return both(piece(zz, qq), lambda k, i: twosem.at[k, d - 1, e - 1, i], target)

    def three(d, cc, zz, target):
        return both(shard(cc, zz), lambda k, i: sibsem.at[k, d, i], target)

    def launch(copies):
        for copy in copies:
            copy.start()
            sends.append(copy)

    for d in range(1, groups):
        to = lax.rem(z + d, groups)
        launch(one(d, z, (core, to, r)))
    launch(three(0, core, z, (sib, z, r)))

    for d in range(1, groups):
        came = lax.rem(z + groups - d, groups)
        remote(
            cond.at[came], condbuf.at[came], (csem.at[0, d - 1], csem.at[1, d - 1]), (core, came, r)
        ).wait_recv()
    for zz in range(groups):
        c = condbuf[zz]
        silu = (c / (1.0 + jnp.exp(-c))).astype(BF16)
        pout[zz, 0:2] = dot(silu, wada[...])
        pout[zz, 2:3] = bias[...]
    pin[core, z] = pout[z]

    hops = [(d, k) for d in range(groups) for k in range(2) if (d, k) != (0, 0)]
    for d, k in hops:
        to = lax.rem(z + d, groups)
        copy = remote(
            pout.at[to],
            pin.at[core, z],
            (psem.at[0, d, k], psem.at[1, d, k]),
            (sib if k else core, to, r),
        )
        copy.start()
        sends.append(copy)

    for d in range(1, groups):
        came = lax.rem(z + groups - d, groups)
        for copy in one(d, came, (core, came, r)):
            copy.wait_recv()
        for e in range(1, 4):
            launch(two(d, e, came, quarter, (core, z, base + lax.rem(quarter + e, 4))))
    for d in range(1, groups):
        came = lax.rem(z + groups - d, groups)
        for e in range(1, 4):
            theirs = lax.rem(quarter + 4 - e, 4)
            for copy in two(d, e, came, theirs, (core, z, base + theirs)):
                copy.wait_recv()
        launch(three(d, core, came, (sib, z, r)))
    for d, k in hops:
        came = lax.rem(z + groups - d, groups)
        remote(
            pout.at[came],
            pin.at[sib if k else core, came],
            (psem.at[0, d, k], psem.at[1, d, k]),
            (sib if k else core, came, r),
        ).wait_recv()
    for d in range(groups):
        came = lax.rem(z + groups - d, groups)
        for copy in three(d, sib, came, (sib, z, r)):
            copy.wait_recv()
    for copy in sends:
        copy.wait_send()


def gather_all(cond, bias, wada, wqkv, wproj, wfc1, wfc2):
    groups = lax.axis_size("group")
    rows = D // groups
    vmem = pl.BlockSpec(memory_space=pltpu.VMEM)
    hbm = pl.BlockSpec(memory_space=pl.ANY)
    dma = pltpu.SemaphoreType.DMA
    return pl.pallas_call(
        gather_kernel,
        out_shape=[
            jax.ShapeDtypeStruct((2, 8, groups, rows, D), BF16),
            jax.ShapeDtypeStruct((2, groups, 4, rows, D), BF16),
            jax.ShapeDtypeStruct((2, groups, 3, 6 * D), F32),
        ],
        in_specs=[vmem] * 3 + [hbm] * 4,
        out_specs=[vmem] * 3,
        scratch_shapes=[
            pltpu.VMEM((groups, 2, rows), F32),
            pltpu.VMEM((groups, 3, 6 * D), F32),
            dma((9,)),
            dma((2, groups - 1)),
            dma((2, groups, 2)),
            dma((2, groups - 1, 2)),
            dma((2, groups - 1, 3, 2)),
            dma((2, groups, 2)),
        ],
        compiler_params=pltpu.CompilerParams(vmem_limit_bytes=40 * 2**20, has_side_effects=True),
        name="gather_all",
    )(cond, bias, wada, wqkv, wproj, wfc1, wfc2)


def reduce_kernel(
    small, wada, g8, gf2,
    fin, every, dsc,
    ra8, raf, sb8, sbf, rb8, rbf, tc, rc, dout,
    allsend, allrecv, asem, bsem, zsem, fsem, dsem,
):
    core, z, r, groups, reps = places()
    quarter = lax.rem(r, 4)
    base = r - quarter
    sib = 1 - core
    total = 2 * groups * reps
    me = (z * reps + r) * 2 + core
    sends = []

    def launch(copies):
        for copy in copies:
            copy.start()
            sends.append(copy)

    def sibling(e, qq):
        return [
            remote(
                g8.at[sib, pl.ds(2 * qq, 2)],
                ra8.at[e],
                (asem.at[0, e, 0], asem.at[1, e, 0]),
                (sib, z, r),
            ),
            remote(
                gf2.at[sib, :, qq], raf.at[e], (asem.at[0, e, 1], asem.at[1, e, 1]), (sib, z, r)
            ),
        ]

    order = (1, 2, 3, 0)
    for e in order:
        launch(sibling(e, lax.rem(quarter + e, 4)))

    def spread(i):
        other = lax.rem(me + i, total)
        there = lax.rem(other, 2)
        chip = other // 2
        return remote(
            small.at[there],
            every.at[me],
            (allsend.at[i], allrecv.at[i]),
            (there, chip // reps, lax.rem(chip, reps)),
        )

    def collect(i):
        other = lax.rem(me + total - i, total)
        chip = other // 2
        return remote(
            small.at[core],
            every.at[other],
            (allsend.at[i], allrecv.at[i]),
            (lax.rem(other, 2), chip // reps, lax.rem(chip, reps)),
        )

    def start_one(i, carry):
        spread(i).start()
        return carry

    lax.fori_loop(1, total, start_one, 0)
    every[me] = small[core]

    def across(e, to):
        return [
            remote(
                sb8.at[e], rb8.at[e - 1], (bsem.at[0, e - 1, 0], bsem.at[1, e - 1, 0]), (core, z, to)
            ),
            remote(
                sbf.at[e], rbf.at[e - 1], (bsem.at[0, e - 1, 1], bsem.at[1, e - 1, 1]), (core, z, to)
            ),
        ]

    for e in order:
        qq = lax.rem(quarter + e, 4)
        for copy in sibling(e, qq):
            copy.wait_recv()
        for i in range(2):
            sb8[e, i] = (g8[core, 2 * qq + i].astype(F32) + ra8[e, i].astype(F32)).astype(BF16)
        sbf[e] = (gf2[core, :, qq].astype(F32) + raf[e].astype(F32)).astype(BF16)
        if e:
            launch(across(e, base + qq))

    def collect_one(i, carry):
        collect(i).wait_recv()
        return carry

    lax.fori_loop(1, total, collect_one, 0)
    for zz in range(groups):
        at = (zz * reps + r) * 2
        rows2 = jnp.concatenate(
            [every[at, :, : 6 * D], every[at + 1, :, : 6 * D]], axis=0
        ).astype(BF16)
        dout[zz] = dot(rows2, wada[...], NT)
    dsc[core, z] = dout[z]
    hops = [(d, k) for d in range(groups) for k in range(2) if (d, k) != (0, 0)]
    for d, k in hops:
        to = lax.rem(z + d, groups)
        launch(
            [
                remote(
                    dout.at[to],
                    dsc.at[core, z],
                    (dsem.at[0, d, k], dsem.at[1, d, k]),
                    (sib if k else core, to, r),
                )
            ]
        )

    for e in range(1, 4):
        theirs = base + lax.rem(quarter + 4 - e, 4)
        for copy in across(e, theirs):
            copy.wait_recv()
    for zz in range(groups):
        for i in range(2):
            t = sb8[0, i, zz].astype(F32)
            for e in range(3):
                t = t + rb8[e, i, zz].astype(F32)
            tc[zz, i] = t.astype(BF16)
        t = sbf[0, zz].astype(F32)
        for e in range(3):
            t = t + rbf[e, zz].astype(F32)
        tc[zz, 2] = t.astype(BF16)

    def along(d, zz, target):
        return remote(tc.at[zz], rc.at[d - 1], (zsem.at[0, d - 1], zsem.at[1, d - 1]), target)

    for d in range(1, groups):
        to = lax.rem(z + d, groups)
        launch([along(d, to, (core, to, r))])
    for d in range(1, groups):
        came = lax.rem(z + groups - d, groups)
        along(d, came, (core, came, r)).wait_recv()
    for i in range(3):
        t = tc[z, i].astype(F32)
        for d in range(groups - 1):
            t = t + rc[d, i].astype(F32)
        fin[quarter, i] = t.astype(BF16)

    def share(e, qq, to):
        return remote(fin.at[qq], fin.at[qq], (fsem.at[0, e - 1], fsem.at[1, e - 1]), (core, z, to))

    for e in range(1, 4):
        launch([share(e, quarter, base + lax.rem(quarter + e, 4))])
    for e in range(1, 4):
        theirs = lax.rem(quarter + 4 - e, 4)
        share(e, theirs, base + theirs).wait_recv()
    for d, k in hops:
        came = lax.rem(z + groups - d, groups)
        who = sib if k else core
        remote(
            dout.at[came],
            dsc.at[who, came],
            (dsem.at[0, d, k], dsem.at[1, d, k]),
            (who, came, r),
        ).wait_recv()

    def finish_one(i, carry):
        spread(i).wait_send()
        return carry

    lax.fori_loop(1, total, finish_one, 0)
    for copy in sends:
        copy.wait_send()


def reduce_all(small, wada, g8, gf2):
    groups, reps = lax.axis_size("group"), lax.axis_size("rep")
    rows = D // groups
    total = 2 * groups * reps
    width = small.shape[-1]
    vmem = pl.BlockSpec(memory_space=pltpu.VMEM)
    dma = pltpu.SemaphoreType.DMA
    fin, every, dsc = pl.pallas_call(
        reduce_kernel,
        out_shape=[
            jax.ShapeDtypeStruct((4, 3, rows, D), BF16),
            jax.ShapeDtypeStruct((total, 1, width), F32),
            jax.ShapeDtypeStruct((2, groups, 2, rows), F32),
        ],
        in_specs=[vmem] * 4,
        out_specs=[vmem] * 3,
        scratch_shapes=[
            pltpu.VMEM((4, 2, groups, rows, D), BF16),
            pltpu.VMEM((4, groups, rows, D), BF16),
            pltpu.VMEM((4, 2, groups, rows, D), BF16),
            pltpu.VMEM((4, groups, rows, D), BF16),
            pltpu.VMEM((3, 2, groups, rows, D), BF16),
            pltpu.VMEM((3, groups, rows, D), BF16),
            pltpu.VMEM((groups, 3, rows, D), BF16),
            pltpu.VMEM((groups - 1, 3, rows, D), BF16),
            pltpu.VMEM((groups, 2, rows), F32),
            dma((total,)),
            dma((total,)),
            dma((2, 4, 2)),
            dma((2, 3, 2)),
            dma((2, groups - 1)),
            dma((2, 3)),
            dma((2, groups, 2)),
        ],
        compiler_params=pltpu.CompilerParams(vmem_limit_bytes=48 * 2**20, has_side_effects=True),
        name="reduce_all",
    )(small, wada, g8.reshape(2, 8, groups, rows, D), gf2.reshape(2, groups, 4, rows, D))
    if reps > 4:
        fin = (lax.psum(fin, "rep").astype(F32) * 0.25).astype(BF16)
    return fin.astype(F32), every, dsc


def swap(value):
    return lax.ppermute(value, "section", [(0, 1), (1, 0)])


def body(
    latents, cond, cotangent, live_count,
    wada, bada, wqkv, wproj, wfc1, bfc1, wfc2,
):
    core = lax.axis_index("section")
    zi = lax.axis_index("group")
    groups = lax.axis_size("group")
    rows = D // groups
    is_first = core == 0

    def pick(a):
        return lax.dynamic_index_in_dim(a, core, 0, keepdims=False)

    live = (live_count[0] > 0).astype(F32)
    x = pick(latents)
    tangent = pick(cotangent)
    cond_cols = jnp.swapaxes(cond.reshape(2, groups, rows), 0, 1)
    bias = jnp.concatenate([bada, bfc1], axis=1).astype(F32)
    bias = jnp.pad(bias, ((0, 0), (0, 6 * D - bias.shape[1])))
    w8, f2, pin = gather_all(
        cond_cols, bias, wada[0], wqkv[0], wproj[0], wfc1[0], wfc2[0].reshape(4, rows, D)
    )
    w8 = w8.reshape(2, 8, D, D)
    f2 = f2.reshape(2, FF, D)
    wide = 6 * D // groups
    high = FF // groups
    bias_ada = pin[:, :, 2, :wide].reshape(2, 6 * D)
    b1 = pin[:, :, 2, wide : wide + high].reshape(2, 1, FF)
    sums = jnp.sum(pin[:, :, :2], axis=1)
    mod = (lax.dynamic_index_in_dim(sums, core, 1, keepdims=False) + bias_ada).reshape(2, 6, D)

    h, z, dlat, dh, dmod, db1, g8, gf2 = relay(
        x, tangent, jnp.broadcast_to(pick(live), (1, 1)), mod, b1, w8, f2
    )

    def rounded(v):
        return v.astype(BF16).astype(F32)

    dmod_low = rounded(dmod.reshape(2, 1, 6 * D))
    silu = jnp.broadcast_to(rounded(jax.nn.silu(pick(cond))), (2, 1, D))
    small = jnp.concatenate([dmod_low, db1, silu], axis=-1)
    fin, every, dsc_all = reduce_all(small, wada[0], g8, gf2)
    every = every[:, 0]
    dmod_all = every[:, : 6 * D].astype(BF16)
    silu_rows = lax.dynamic_slice_in_dim(every[:, 6 * D + FF :], zi * rows, rows, 1).astype(BF16)
    grad_ada = lax.dot_general(silu_rows, dmod_all, TN, preferred_element_type=F32)
    sums = jnp.sum(every[:, : 6 * D + FF], axis=0)
    grad_bada = lax.dynamic_slice_in_dim(sums[: 6 * D], zi * wide, wide, 0)
    grad_bfc1 = lax.dynamic_slice_in_dim(sums[6 * D :], zi * high, high, 0)
    dsc = jnp.swapaxes(dsc_all, 1, 2).reshape(2, 2, D)
    sig = jax.nn.sigmoid(cond)
    dc = dsc * (sig * (1.0 + cond * (1.0 - sig)))
    low = dc[1].astype(BF16).astype(F32)
    cond_grads = jnp.where(is_first, dc[0] + low, low)

    chunks = fin[:, :2].reshape(8, rows, D)

    def joined(j, n):
        return jnp.swapaxes(chunks[j : j + n], 0, 1).reshape(1, rows, n * D)

    wq, wp, w1 = joined(0, 3), joined(3, 1), joined(4, 4)
    w2 = fin[:, 2].reshape(1, 4 * rows, D)

    sent = swap((jnp.where(is_first, z, h), jnp.where(is_first, dh, dlat.astype(BF16))))
    keep = jnp.where(is_first, h, z)
    section_outputs = jnp.where(
        is_first, jnp.stack([keep, sent[0]]), jnp.stack([sent[0], keep])
    )
    kept_grad = jnp.where(is_first, dlat, dh.astype(F32))
    got = sent[1].astype(F32)
    input_grads = jnp.where(is_first, jnp.stack([kept_grad, got]), jnp.stack([got, kept_grad]))
    return (
        section_outputs[None],
        input_grads[None],
        cond_grads[None],
        grad_ada[None],
        grad_bada[None],
        wq,
        wp,
        w1,
        grad_bfc1[None],
        w2,
    )


def solution(mesh):
    data = P(("group", "rep"))
    weight = P("section", "group")
    return jax.shard_map(
        body,
        mesh=mesh,
        in_specs=(data,) * 4 + (weight,) * 7,
        out_specs=(P("section", ("group", "rep")),) * 3 + (weight,) * 7,
        check_vma=False,
    )
```
